32 devices in a mesh: groups: 2 (over x), seq: 16 (over z, y, core).
Axes of the slice: x: 2, y: 2, z: 4, core: 2. Of those that a mesh axis runs over, the one named last changes fastest.
Arguments:
- hidden_in: bfloat16 [16384, 768], P(('groups', 'seq')), parts along dimension 0
- ln_gain: float32 [2, 768], replicated, may hold values from 0.5 to 1.5
- w_qkv: bfloat16 [2, 768, 2304], replicated
- w_out: bfloat16 [2, 768, 768], replicated, may hold values from -0.21875 to 0.21875
- final_gain: float32 [768], replicated, may hold values from 0.5 to 1.5
- w_heads: bfloat16 [768, 512], replicated
- actions: int32 [16384], P(('groups', 'seq')), parts along dimension 0, may hold values from 0 to 255
- propensity: int32 [16384], P(('groups', 'seq')), parts along dimension 0, may hold values from 1024 to 65535
- logged_reward: float32 [16384], P(('groups', 'seq')), parts along dimension 0, may hold values from -6 to 6
- switch_index: int32 [2], P('groups'), parts along dimension 0, may hold values from 2 to 9
Outputs:
- rewards: float32 [16384], P(('groups', 'seq')), parts along dimension 0
- dr_terms: float32 [16384], P(('groups', 'seq')), parts along dimension 0
The draws below stay inside these ranges and needn't reach their ends.
There are 2 independent parts, one for each index of `groups`. The reference program is written for one: setup_inputs(seed, part) draws one part's arguments, and reference() takes and returns one part's arrays. A program takes and returns all parts, laid end to end along the dimension named above; an argument that names none is the same for every part. Nothing has to cross between parts.
All inputs are finite; a program needn't handle non-finite values.
Results may differ from the reference program's by a relative error of at most 0.03.
Values may be sent and summed in bfloat16 or wider, within the bound.
A program may use at most 128 MiB of HBM per device.

```python
import jax
import jax.numpy as jnp
from jax import lax

D = 768
HEADS = 12
HEAD = 64
HALF = 256
PROMPT = 256
ACTIONS = 256
LAYERS = 2
TOK_DEV = 512
SEQLEN = 8192


def draw_hidden_in(key, part):
    key_noise = jax.random.fold_in(key, 11)
    noise_part = jax.random.normal(key_noise, (SEQLEN, D), jnp.float32)
    result = noise_part
    return result.astype(jnp.bfloat16)


def draw_w_qkv(key, part):
    key_base = jax.random.fold_in(key, 21)
    base_draw = jax.random.normal(key_base, (LAYERS, D, 3 * D), jnp.float32) * D ** (-0.5)
    return base_draw.astype(jnp.bfloat16)


def draw_w_heads(key, part):
    key_policy = jax.random.fold_in(key, 31)
    key_reward = jax.random.fold_in(key, 32)
    policy_part = jax.random.normal(key_policy, (D, ACTIONS), jnp.float32) * (3.0 * D ** (-0.5))
    reward_part = jax.random.normal(key_reward, (D, ACTIONS), jnp.float32) * D ** (-0.5)
    return jnp.concatenate([policy_part, reward_part], axis=-1).astype(jnp.bfloat16)


def place_ends(array, stream_key, least, largest):
    extent = array.shape
    place = [jax.random.randint(jax.random.fold_in(stream_key, axis), (), 0, extent[axis]) for axis in range(len(extent))]
    array = array.at[tuple(place)].set(least)
    longest = extent.index(max(extent))
    place[longest] = (place[longest] + 1) % extent[longest]
    return array.at[tuple(place)].set(largest)


def block_scale(rng, dims, pieces, least, high):
    def one(axis_at, shards_of):
        steps = jax.random.uniform(jax.random.fold_in(jax.random.fold_in(rng, 6), axis_at), (shards_of,), jnp.float32, least / len(pieces), high / len(pieces))
        return jnp.repeat(jnp.exp(steps), dims[axis_at] // shards_of).reshape((-1,) + (1,) * (len(dims) - axis_at - 1))

    factor_of = one(*pieces[0])
    for cut in pieces[1:]:
        factor_of = factor_of * one(*cut)
    return factor_of


def scatter_about(key, shape, deviation, most, shards=(), kind=jnp.bfloat16):
    loudness = block_scale(key, shape, shards, -0.22, 0.18) if shards else 1.0
    values = jax.random.normal(key, shape, jnp.float32) * deviation * loudness
    return jnp.minimum(jnp.maximum(values, -most), most).astype(kind)


def setup_inputs(seed: int = 0, part: int = 0) -> dict:
    key_of = jax.random.split(jax.random.key(seed), 11)
    own_keys = jax.random.split(jax.random.fold_in(key_of[10], part), 11)
    return {
        "hidden_in": draw_hidden_in(jax.random.fold_in(jax.random.fold_in(key_of[10], part), 71), part),
        "ln_gain": jnp.clip(1.0 + 0.1 * jax.random.normal(key_of[1], (LAYERS, D), jnp.float32), 0.5, 1.5),
        "w_qkv": draw_w_qkv(jax.random.fold_in(key_of[10], 71), part),
        "w_out": scatter_about(key_of[3], (LAYERS, D, D), D ** -0.5, 0.21875),
        "final_gain": jnp.clip(1.0 + 0.1 * jax.random.normal(key_of[4], (D,), jnp.float32), 0.5, 1.5),
        "w_heads": draw_w_heads(jax.random.fold_in(key_of[10], 71), part),
        "actions": place_ends(jax.random.randint(own_keys[6], (SEQLEN,), 0, ACTIONS), jax.random.fold_in(own_keys[6], 1), 0, ACTIONS - 1).astype(jnp.int32),
        "propensity": place_ends(jax.random.randint(own_keys[7], (SEQLEN,), 1024, 65536), jax.random.fold_in(own_keys[7], 1), 1024, 65535).astype(jnp.int32),
        "logged_reward": scatter_about(own_keys[8], (SEQLEN,), 1.0, 6.0, ((0, 16),), jnp.float32),
        "switch_index": jax.random.randint(own_keys[9], (1,), 2, 10).astype(jnp.int32),
    }


def layer_norm(hidden_state, gain_row):
    values_f = hidden_state.astype(jnp.float32)
    row_mean = lax.optimization_barrier(jnp.mean(values_f, axis=-1, keepdims=True))
    centred = values_f - row_mean
    row_var = lax.optimization_barrier(jnp.mean(centred * centred, axis=-1, keepdims=True))
    return (centred * lax.rsqrt(row_var + 1e-05) * gain_row).astype(jnp.bfloat16)

def attend_block(query_block, key_block, value_block, prompt_keys, prompt_values, row_start, total_len):
    block_rows = query_block.shape[0]
    band_width = key_block.shape[0]
    query_f = query_block.astype(jnp.float32)
    band_scores = jnp.einsum('qhe,khe->hqk', query_f, key_block.astype(jnp.float32))
    prompt_scores = jnp.einsum('qhe,khe->hqk', query_f, prompt_keys.astype(jnp.float32))
    query_pos = row_start + jnp.arange(block_rows, dtype=jnp.int32)
    key_pos = row_start - HALF + jnp.arange(band_width, dtype=jnp.int32)
    prompt_pos = jnp.arange(PROMPT, dtype=jnp.int32)
    band_mask = (jnp.abs(key_pos[None, :] - query_pos[:, None]) <= HALF) & (key_pos[None, :] >= 0) & (key_pos[None, :] < total_len)
    prompt_mask = jnp.abs(prompt_pos[None, :] - query_pos[:, None]) > HALF
    scores = jnp.concatenate([jnp.where(prompt_mask[None], prompt_scores, -1e+30), jnp.where(band_mask[None], band_scores, -1e+30)], axis=-1)
    row_max = lax.optimization_barrier(jnp.max(scores, axis=-1, keepdims=True))
    exps = jnp.exp(scores - row_max)
    attn_probs = (exps / lax.optimization_barrier(jnp.sum(exps, axis=-1, keepdims=True))).astype(jnp.bfloat16)
    value_rows = jnp.concatenate([prompt_values, value_block], axis=0)
    attn_out = jnp.einsum('hqk,khe->qhe', attn_probs.astype(jnp.float32), value_rows.astype(jnp.float32))
    return attn_out.reshape(block_rows, HEADS * HEAD).astype(jnp.bfloat16)

def reference(hidden_in, ln_gain, w_qkv, w_out, final_gain, w_heads, actions, propensity, logged_reward, switch_index):
    total_len = hidden_in.shape[0]
    feat_width = hidden_in.shape[1]
    block_rows = min(256, TOK_DEV)
    block_count = total_len // block_rows
    hidden_state = hidden_in
    for layer_idx in range(LAYERS):
        normed = layer_norm(hidden_state, ln_gain[layer_idx])
        projected = jnp.dot(normed, w_qkv[layer_idx], preferred_element_type=jnp.float32)
        queries = (projected[:, :feat_width] * 0.125).astype(jnp.bfloat16).reshape(total_len, HEADS, HEAD)
        keys_all = projected[:, feat_width:2 * feat_width].astype(jnp.bfloat16).reshape(total_len, HEADS, HEAD)
        values_all = projected[:, 2 * feat_width:].astype(jnp.bfloat16).reshape(total_len, HEADS, HEAD)
        prompt_keys = keys_all[:PROMPT]
        prompt_values = values_all[:PROMPT]
        pad_keys = jnp.pad(keys_all, ((HALF, HALF), (0, 0), (0, 0)))
        pad_values = jnp.pad(values_all, ((HALF, HALF), (0, 0), (0, 0)))

        def one_block(block_idx):
            row_start = block_idx * block_rows
            return attend_block(lax.dynamic_slice_in_dim(queries, row_start, block_rows), lax.dynamic_slice_in_dim(pad_keys, row_start, block_rows + 2 * HALF), lax.dynamic_slice_in_dim(pad_values, row_start, block_rows + 2 * HALF), prompt_keys, prompt_values, row_start, total_len)
        attended = lax.map(one_block, jnp.arange(block_count, dtype=jnp.int32)).reshape(total_len, feat_width)
        projection = jnp.dot(attended, w_out[layer_idx], preferred_element_type=jnp.float32)
        hidden_state = (hidden_state.astype(jnp.float32) + projection).astype(jnp.bfloat16)
    final = layer_norm(hidden_state, final_gain)
    head_out = jnp.dot(final, w_heads, preferred_element_type=jnp.float32)
    logits = head_out[:, :ACTIONS]
    reward_table = head_out[:, ACTIONS:]
    logit_max = lax.optimization_barrier(jnp.max(logits, axis=-1, keepdims=True))
    exps = jnp.exp(logits - logit_max)
    policy = exps / lax.optimization_barrier(jnp.sum(exps, axis=-1, keepdims=True))
    chosen = actions[:, None] == jnp.arange(ACTIONS, dtype=jnp.int32)[None, :]
    rewards = lax.optimization_barrier(jnp.sum(jnp.where(chosen, reward_table, 0.0), axis=-1))
    chosen_prob = lax.optimization_barrier(jnp.sum(jnp.where(chosen, policy, 0.0), axis=-1))
    direct = lax.optimization_barrier(jnp.sum(policy * reward_table, axis=-1))
    logged_prob = propensity.astype(jnp.float32) / 65536.0
    cutoff = 0.5 * switch_index[0].astype(jnp.float32)
    dr_terms = direct + jnp.minimum(chosen_prob / logged_prob, cutoff) * (logged_reward - rewards)
    return (rewards, dr_terms)
```

```python
import functools

import jax
import jax.numpy as jnp
from jax import lax
from jax.experimental import pallas as pl
from jax.experimental.pallas import tpu as pltpu
from jax.sharding import PartitionSpec as P

HEADS = 12
HEAD = 64
HALF = 256
PROMPT = 256
ACTIONS = 256
LAYERS = 2
BLOCK = 256
TILE = 256
PAIR = 2 * HEAD
CHUNKS = 4
MESH = pl.DeviceIdType.MESH
AT_PROMPT, AT_BEFORE, AT_OWN = 0, PROMPT, PROMPT + HALF
LOG2E = 1.4426950408889634


def norm_rows(rows, gain_row):
    row_mean = jnp.mean(rows, axis=-1, keepdims=True)
    centred = rows - row_mean
    row_var = jnp.mean(centred * centred, axis=-1, keepdims=True)
    return (centred * lax.rsqrt(row_var + 1e-05) * gain_row).astype(jnp.bfloat16)


def kernel(
    n,
    hidden_ref,
    gain_ref,
    final_gain_ref,
    actions_ref,
    propensity_ref,
    logged_ref,
    switch_ref,
    w_qkv_hbm,
    w_out_hbm,
    w_heads_hbm,
    rewards_ref,
    dr_ref,
    w_qkv,
    w_out,
    w_heads,
    states,
    q_s,
    k_s,
    va_s,
    vb_s,
    att_s,
    h_s,
    bias_s,
    load_sem,
    halo_send,
    halo_recv,
    tree_send,
    tree_recv,
):
    tok_rows, width = hidden_ref.shape
    at_after = AT_OWN + tok_rows
    tiles = width // TILE
    pairs = HEADS // 2
    me = lax.axis_index("seq")
    chip, core = me // 2, me % 2
    depth = chip // 2 + chip % 2 + core
    points = CHUNKS + (n // 2 - 1) // 2 + 2
    parent = jnp.where(core == 1, me - 1, jnp.where(chip % 2 == 1, me - 2, me - 4))
    even = core == 0
    children = (
        (me + 4, even & (chip % 2 == 0) & (me + 4 < n)),
        (me + 2, even & (chip % 2 == 0) & (me + 2 < n)),
        (me + 1, even & (me + 1 < n)),
    )
    has_left, has_right, has_parent = me > 0, me < n - 1, me > 0

    loads = [pltpu.make_async_copy(w_qkv_hbm.at[0], w_qkv.at[0], load_sem.at[0])]
    loads.append(pltpu.make_async_copy(w_out_hbm.at[0], w_out.at[0], load_sem.at[1]))
    loads.append(pltpu.make_async_copy(w_qkv_hbm.at[1], w_qkv.at[1], load_sem.at[2]))
    loads.append(pltpu.make_async_copy(w_out_hbm.at[1], w_out.at[1], load_sem.at[3]))
    loads.append(pltpu.make_async_copy(w_heads_hbm, w_heads, load_sem.at[4]))
    for load in loads:
        load.start()

    barrier = pltpu.get_barrier_semaphore()
    partners = ((me - 1, has_left), (me + 1, has_right), (parent, has_parent)) + children
    for partner, there in partners:

        @pl.when(there)
        def _(partner=partner):
            pl.semaphore_signal(barrier, inc=1, device_id={"seq": partner}, device_id_type=MESH)

    def halo(layer, side):
        src = AT_OWN if side == 0 else at_after - HALF
        dst = at_after if side == 0 else AT_BEFORE
        return pltpu.make_async_remote_copy(
            src_ref=states.at[layer, pl.ds(src, HALF)],
            dst_ref=states.at[layer, pl.ds(dst, HALF)],
            send_sem=halo_send.at[layer, side],
            recv_sem=halo_recv.at[layer, side],
            device_id={"seq": me - 1 if side == 0 else me + 1},
            device_id_type=MESH,
        )

    def piece(layer, chunk, slot, target):
        rows = PROMPT // CHUNKS
        part = states.at[layer, pl.ds(pl.multiple_of(chunk * rows, rows), rows)]
        return pltpu.make_async_remote_copy(
            src_ref=part,
            dst_ref=part,
            send_sem=tree_send.at[layer, slot, chunk],
            recv_sem=tree_recv.at[layer, chunk],
            device_id={"seq": target},
            device_id_type=MESH,
        )

    def pass_on(layer, point):
        chunk = point - depth

        @pl.when((chunk >= 0) & (chunk < CHUNKS))
        def _():
            @pl.when(has_parent)
            def _():
                piece(layer, chunk, 0, parent).wait_recv()

            for slot, (child, there) in enumerate(children):

                @pl.when(there)
                def _(slot=slot, child=child):
                    piece(layer, chunk, slot, child).start()

    def finish_passing(layer, done):
        if done < points:

            @pl.loop(done, points)
            def _(point):
                pass_on(layer, point)

    def wait_halo(layer, side):
        @pl.when(has_right if side == 0 else has_left)
        def _():
            halo(layer, side).wait_recv()

    def send_halo(layer, side):
        @pl.when(has_left if side == 0 else has_right)
        def _():
            halo(layer, side).start()

    def start_prompt(layer):
        @pl.when(me == 0)
        def _():
            states[layer, pl.ds(AT_PROMPT, PROMPT), :] = states[layer, pl.ds(AT_OWN, PROMPT), :]

    lane = lax.broadcasted_iota(jnp.int32, (1, PAIR), 1)
    first_half = lane < HEAD

    def project_kv(layer, row, rows, j):
        x = states[layer, pl.ds(row, rows), :]
        for which in (1, 2):
            at = pl.multiple_of(which * width + j * TILE, TILE)
            out = jnp.dot(x, w_qkv[layer, :, pl.ds(at, TILE)], preferred_element_type=jnp.float32)
            for part in range(TILE // PAIR):
                cols = out[:, part * PAIR : (part + 1) * PAIR]
                slot = j * (TILE // PAIR) + part
                if which == 1:
                    k_s[slot, pl.ds(row, rows), :] = cols.astype(jnp.bfloat16)
                else:
                    va_s[slot, pl.ds(row, rows), :] = jnp.where(first_half, cols, 1.0).astype(
                        jnp.bfloat16
                    )
                    vb_s[slot, pl.ds(row, rows), :] = jnp.where(first_half, 1.0, cols).astype(
                        jnp.bfloat16
                    )

    def project_q(layer, j):
        at = pl.multiple_of(j * TILE, TILE)
        x = states[layer, pl.ds(AT_OWN, tok_rows), :]
        out = jnp.dot(x, w_qkv[layer, :, pl.ds(at, TILE)], preferred_element_type=jnp.float32)
        out = out * (0.125 * LOG2E)
        for part in range(TILE // PAIR):
            cols = out[:, part * PAIR : (part + 1) * PAIR]
            slot = j * (TILE // PAIR) + part
            qa = jnp.where(first_half, cols, 0.0).astype(jnp.bfloat16)
            qb = jnp.where(first_half, 0.0, cols).astype(jnp.bfloat16)
            for block in range(tok_rows // BLOCK):
                rows = slice(block * BLOCK, (block + 1) * BLOCK)
                q_s[slot, block, pl.ds(0, BLOCK), :] = qa[rows]
                q_s[slot, block, pl.ds(BLOCK, BLOCK), :] = qb[rows]

    def attend(layer, block, pair):
        band = AT_BEFORE + block * BLOCK
        starts = (AT_PROMPT, band, band + BLOCK, band + 2 * BLOCK)
        q = q_s[pair, block]
        scores = []
        for which, start in enumerate(starts):
            s = lax.dot_general(
                q,
                k_s[pair, pl.ds(start, BLOCK), :],
                (((1,), (1,)), ((), ())),
                preferred_element_type=jnp.float32,
            )
            if which != 2:
                bias = bias_s[block, min(which, 2)]
                s = jnp.concatenate([s[:BLOCK] + bias, s[BLOCK:] + bias], axis=0)
            scores.append(s)
        top = jnp.maximum(
            jnp.maximum(scores[0], scores[1]), jnp.maximum(scores[2], scores[3])
        )
        top = jnp.max(top, axis=-1, keepdims=True)
        out_a = jnp.zeros((BLOCK, PAIR), jnp.float32)
        out_b = jnp.zeros((BLOCK, PAIR), jnp.float32)
        for s, start in zip(scores, starts):
            p = jnp.exp2(s - top).astype(jnp.bfloat16)
            out_a += jnp.dot(
                p[:BLOCK], va_s[pair, pl.ds(start, BLOCK), :], preferred_element_type=jnp.float32
            )
            out_b += jnp.dot(
                p[BLOCK:], vb_s[pair, pl.ds(start, BLOCK), :], preferred_element_type=jnp.float32
            )
        total = pltpu.roll(jnp.where(first_half, out_b, out_a), HEAD, 1)
        att = jnp.where(first_half, out_a, out_b) / total
        att_s[:, pl.ds(pl.multiple_of(pair * PAIR, PAIR), PAIR)] = att.astype(jnp.bfloat16)

    def add_out(layer, block):
        rows = pl.ds(block * BLOCK, BLOCK)
        source = hidden_ref if layer == 0 else h_s
        old = source[rows, :].astype(jnp.float32)
        new = old + jnp.dot(att_s[...], w_out[layer], preferred_element_type=jnp.float32)
        return new.astype(jnp.bfloat16)

    def head(block, h):
        rows = pl.ds(block * BLOCK, BLOCK)
        final = norm_rows(h.astype(jnp.float32), final_gain_ref[...])
        out = jnp.dot(final, w_heads[...], preferred_element_type=jnp.float32)
        logits, table = out[:, :ACTIONS], out[:, ACTIONS:]
        exps = jnp.exp(logits - jnp.max(logits, axis=-1, keepdims=True))
        norm = jnp.sum(exps, axis=-1, keepdims=True)
        action = jnp.broadcast_to(actions_ref[:, rows].astype(jnp.float32), (128, BLOCK))
        action = jnp.transpose(action)[:, :1].astype(jnp.int32)
        chosen = action == lax.broadcasted_iota(jnp.int32, (1, ACTIONS), 1)
        reward = jnp.sum(jnp.where(chosen, table, 0.0), axis=-1, keepdims=True)
        prob = jnp.sum(jnp.where(chosen, exps, 0.0), axis=-1, keepdims=True) / norm
        direct = jnp.sum(exps * table, axis=-1, keepdims=True) / norm
        place = lax.broadcasted_iota(jnp.int32, (1, 128), 1)
        packed = jnp.where(place == 0, reward, jnp.where(place == 1, prob, direct))
        packed = jnp.transpose(packed)
        reward, prob, direct = packed[0:1], packed[1:2], packed[2:3]
        logged_prob = propensity_ref[:, rows].astype(jnp.float32) / 65536.0
        cutoff = 0.5 * switch_ref[0].astype(jnp.float32)
        weight = jnp.minimum(prob / logged_prob, cutoff)
        rewards_ref[:, rows] = reward
        dr_ref[:, rows] = direct + weight * (logged_ref[:, rows] - reward)

    def own_block(block):
        return pl.ds(AT_OWN + block * BLOCK, BLOCK)

    for block in range(2):
        rows = hidden_ref[pl.ds(block * BLOCK, BLOCK), :].astype(jnp.float32)
        states[0, own_block(block), :] = norm_rows(rows, gain_ref[0:1, :])

    count = jnp.int32(0)
    for _, there in partners:
        count = count + jnp.where(there, 1, 0)
    pl.semaphore_wait(barrier, count)

    start_prompt(0)
    send_halo(0, 0)
    send_halo(0, 1)

    @pl.when(jnp.logical_not(has_left))
    def _():
        for layer in range(LAYERS):
            states[layer, pl.ds(AT_BEFORE, HALF), :] = jnp.zeros((HALF, width), jnp.bfloat16)

    @pl.when(jnp.logical_not(has_right))
    def _():
        for layer in range(LAYERS):
            states[layer, pl.ds(at_after, HALF), :] = jnp.zeros((HALF, width), jnp.bfloat16)

    row = lax.broadcasted_iota(jnp.int32, (BLOCK, BLOCK), 0)
    col = lax.broadcasted_iota(jnp.int32, (BLOCK, BLOCK), 1)
    for block in range(2):
        place = me * 2 + block
        off = row - col
        seen = (
            off + place * BLOCK > HALF,
            (off <= 0) & (place > 0),
            (off >= 0) & (place < 2 * n - 1),
        )
        for which, ok in enumerate(seen):
            bias_s[block, which] = jnp.where(ok, 0.0, -1e30)

    loads[0].wait()

    @pl.loop(0, tiles)
    def _(j):
        pass_on(0, j)
        project_kv(0, AT_OWN, tok_rows, j)
        project_q(0, j)

    wait_halo(0, 0)

    @pl.loop(0, tiles)
    def _(j):
        pass_on(0, j + tiles)
        project_kv(0, at_after, HALF, j)

    wait_halo(0, 1)

    @pl.loop(0, tiles)
    def _(j):
        pass_on(0, j + 2 * tiles)
        project_kv(0, AT_BEFORE, HALF, j)

    finish_passing(0, 3 * tiles)

    @pl.loop(0, tiles)
    def _(j):
        project_kv(0, AT_PROMPT, PROMPT, j)

    @pl.loop(0, pairs)
    def _(pair):
        attend(0, 0, pair)

    loads[1].wait()
    h = add_out(0, 0)
    h_s[pl.ds(0, BLOCK), :] = h
    states[1, own_block(0), :] = norm_rows(h.astype(jnp.float32), gain_ref[1:2, :])
    send_halo(1, 0)
    start_prompt(1)

    @pl.loop(0, pairs)
    def _(pair):
        pass_on(1, pair)
        attend(0, 1, pair)

    h = add_out(0, 1)
    h_s[pl.ds(BLOCK, BLOCK), :] = h
    states[1, own_block(1), :] = norm_rows(h.astype(jnp.float32), gain_ref[1:2, :])
    send_halo(1, 1)

    loads[2].wait()

    @pl.loop(0, tiles)
    def _(j):
        pass_on(1, j + pairs)
        project_kv(1, AT_OWN, tok_rows, j)
        project_q(1, j)

    wait_halo(1, 0)

    @pl.loop(0, tiles)
    def _(j):
        project_kv(1, at_after, HALF, j)

    finish_passing(1, pairs + tiles)

    @pl.loop(0, tiles)
    def _(j):
        project_kv(1, AT_PROMPT, PROMPT, j)

    @pl.loop(0, pairs)
    def _(pair):
        attend(1, 1, pair)

    loads[3].wait()
    loads[4].wait()
    head(1, add_out(1, 1))
    wait_halo(1, 1)

    @pl.loop(0, tiles)
    def _(j):
        project_kv(1, AT_BEFORE, HALF, j)

    @pl.loop(0, pairs)
    def _(pair):
        attend(1, 0, pair)

    head(0, add_out(1, 0))

    for layer in range(LAYERS):
        for side, there in ((0, has_left), (1, has_right)):

            @pl.when(there)
            def _(layer=layer, side=side):
                halo(layer, side).wait_send()

        for slot, (child, there) in enumerate(children):

            @pl.when(there)
            def _(layer=layer, slot=slot, child=child):
                for chunk in range(CHUNKS):
                    piece(layer, chunk, slot, child).wait_send()


def per_device(
    hidden_in,
    ln_gain,
    w_qkv,
    w_out,
    final_gain,
    w_heads,
    actions,
    propensity,
    logged_reward,
    switch_index,
):
    n = lax.axis_size("seq")
    tok_rows, width = hidden_in.shape
    gathered = tok_rows + 2 * HALF + PROMPT
    pairs = HEADS // 2
    vmem = pl.BlockSpec(memory_space=pltpu.VMEM)
    smem = pl.BlockSpec(memory_space=pltpu.SMEM)
    hbm = pl.BlockSpec(memory_space=pl.ANY)
    line = jax.ShapeDtypeStruct((1, tok_rows), jnp.float32)
    bf16 = jnp.bfloat16
    rewards, dr_terms = pl.pallas_call(
        functools.partial(kernel, n),
        out_shape=(line, line),
        in_specs=[vmem] * 6 + [smem] + [hbm] * 3,
        out_specs=(vmem, vmem),
        scratch_shapes=[
            pltpu.VMEM(w_qkv.shape, bf16),
            pltpu.VMEM(w_out.shape, bf16),
            pltpu.VMEM(w_heads.shape, bf16),
            pltpu.VMEM((LAYERS, gathered, width), bf16),
            pltpu.VMEM((pairs, tok_rows // BLOCK, 2 * BLOCK, PAIR), bf16),
            pltpu.VMEM((pairs, gathered, PAIR), bf16),
            pltpu.VMEM((pairs, gathered, PAIR), bf16),
            pltpu.VMEM((pairs, gathered, PAIR), bf16),
            pltpu.VMEM((BLOCK, width), bf16),
            pltpu.VMEM((tok_rows, width), bf16),
            pltpu.VMEM((tok_rows // BLOCK, 3, BLOCK, BLOCK), jnp.float32),
            pltpu.SemaphoreType.DMA((5,)),
            pltpu.SemaphoreType.DMA((LAYERS, 2)),
            pltpu.SemaphoreType.DMA((LAYERS, 2)),
            pltpu.SemaphoreType.DMA((LAYERS, 3, CHUNKS)),
            pltpu.SemaphoreType.DMA((LAYERS, CHUNKS)),
        ],
        compiler_params=pltpu.CompilerParams(
            collective_id=0, has_side_effects=True, vmem_limit_bytes=56 * 2**20
        ),
    )(
        hidden_in,
        ln_gain,
        final_gain.reshape(1, width),
        actions.reshape(1, tok_rows),
        propensity.reshape(1, tok_rows),
        logged_reward.reshape(1, tok_rows),
        switch_index,
        w_qkv,
        w_out,
        w_heads,
    )
    return rewards.reshape(tok_rows), dr_terms.reshape(tok_rows)


def solution(mesh):
    placed = (
        P(("groups", "seq"), None),
        P(),
        P(),
        P(),
        P(),
        P(),
        P(("groups", "seq")),
        P(("groups", "seq")),
        P(("groups", "seq")),
        P("groups"),
    )
    return jax.shard_map(
        per_device,
        mesh=mesh,
        in_specs=placed,
        out_specs=(P(("groups", "seq")), P(("groups", "seq"))),
        check_vma=False,
    )
```

```python
import functools

import jax
import jax.numpy as jnp
from jax import lax
from jax.experimental import pallas as pl
from jax.experimental.pallas import tpu as pltpu
from jax.sharding import PartitionSpec as P

HEADS = 12
HEAD = 64
HALF = 256
PROMPT = 256
ACTIONS = 256
LAYERS = 2
BLOCK = 256
TILE = 256
PAIR = 2 * HEAD
CHUNKS = 4
GROUP = 3
BAND_GROUP = 2
MESH = pl.DeviceIdType.MESH
AT_PROMPT, AT_BEFORE, AT_OWN = 0, PROMPT, PROMPT + HALF
LOG2E = 1.4426950408889634


def norm_rows(rows, gain_row):
    row_mean = jnp.mean(rows, axis=-1, keepdims=True)
    centred = rows - row_mean
    row_var = jnp.mean(centred * centred, axis=-1, keepdims=True)
    return (centred * lax.rsqrt(row_var + 1e-05) * gain_row).astype(jnp.bfloat16)


def kernel(
    n,
    hidden_ref,
    gain_ref,
    final_gain_ref,
    actions_ref,
    propensity_ref,
    logged_ref,
    switch_ref,
    w_qkv_hbm,
    w_out_hbm,
    w_heads_hbm,
    out_ref,
    w_qkv,
    w_out,
    w_heads,
    states,
    q_s,
    k_s,
    va_s,
    vb_s,
    att_s,
    h_s,
    bias_s,
    part_s,
    top_s,
    load_sem,
    halo_send,
    halo_recv,
    tree_send,
    tree_recv,
):
    tok_rows, width = hidden_ref.shape
    at_after = AT_OWN + tok_rows
    tiles = width // TILE
    pairs = HEADS // 2
    me = lax.axis_index("seq")
    chip, core = me // 2, me % 2
    depth = chip // 2 + chip % 2 + core
    points = (n // 2 - 1) // 2 + 4
    turn = jnp.where(core == 1, points - 1, depth)
    parent = jnp.where(core == 1, me - 1, jnp.where(chip == 1, me - 2, me - 4))
    even = core == 0
    children = (
        (me + 4, even & (me + 4 < n)),
        (me + 2, (me == 0) & (me + 2 < n)),
        (me + 1, even & (me + 1 < n)),
    )
    has_left, has_right, has_parent = me > 0, me < n - 1, me > 0

    loads = [pltpu.make_async_copy(w_qkv_hbm.at[0], w_qkv.at[0], load_sem.at[0])]
    loads.append(pltpu.make_async_copy(w_out_hbm.at[0], w_out.at[0], load_sem.at[1]))
    loads.append(pltpu.make_async_copy(w_qkv_hbm.at[1], w_qkv.at[1], load_sem.at[2]))
    loads.append(pltpu.make_async_copy(w_out_hbm.at[1], w_out.at[1], load_sem.at[3]))
    loads.append(pltpu.make_async_copy(w_heads_hbm, w_heads, load_sem.at[4]))
    for load in loads:
        load.start()

    barrier = pltpu.get_barrier_semaphore()
    partners = ((me - 1, has_left), (me + 1, has_right), (parent, has_parent)) + children
    for partner, there in partners:

        @pl.when(there)
        def _(partner=partner):
            pl.semaphore_signal(barrier, inc=1, device_id={"seq": partner}, device_id_type=MESH)

    def halo(layer, side):
        src = AT_OWN if side == 0 else at_after - HALF
        dst = at_after if side == 0 else AT_BEFORE
        return pltpu.make_async_remote_copy(
            src_ref=states.at[layer, pl.ds(src, HALF)],
            dst_ref=states.at[layer, pl.ds(dst, HALF)],
            send_sem=halo_send.at[layer, side],
            recv_sem=halo_recv.at[layer, side],
            device_id={"seq": me - 1 if side == 0 else me + 1},
            device_id_type=MESH,
        )

    def piece(layer, chunk, slot, target):
        rows = PROMPT // CHUNKS
        part = states.at[layer, pl.ds(pl.multiple_of(chunk * rows, rows), rows)]
        return pltpu.make_async_remote_copy(
            src_ref=part,
            dst_ref=part,
            send_sem=tree_send.at[layer, slot, chunk],
            recv_sem=tree_recv.at[layer, chunk],
            device_id={"seq": target},
            device_id_type=MESH,
        )

    def send_piece(layer, chunk):
        for slot, (child, there) in enumerate(children):

            @pl.when(there)
            def _(slot=slot, child=child):
                piece(layer, chunk, slot, child).start()

    def pass_on(layer, point):
        @pl.when(has_parent & (turn == point))
        def _():
            @pl.loop(0, CHUNKS)
            def _(chunk):
                piece(layer, chunk, 0, parent).wait_recv()
                send_piece(layer, chunk)

    def finish_passing(layer, done):
        if done < points:

            @pl.loop(done, points)
            def _(point):
                pass_on(layer, point)

    def wait_halo(layer, side):
        @pl.when(has_right if side == 0 else has_left)
        def _():
            halo(layer, side).wait_recv()

    def send_halo(layer, side):
        @pl.when(has_left if side == 0 else has_right)
        def _():
            halo(layer, side).start()

    def start_prompt(layer):
        @pl.when(me == 0)
        def _():
            states[layer, pl.ds(AT_PROMPT, PROMPT), :] = states[layer, pl.ds(AT_OWN, PROMPT), :]

            @pl.loop(0, CHUNKS)
            def _(chunk):
                send_piece(layer, chunk)

    lane = lax.broadcasted_iota(jnp.int32, (1, PAIR), 1)
    first_half = lane < HEAD

    def project_kv(layer, row, rows, j):
        x = states[layer, pl.ds(row, rows), :]
        for which in (1, 2):
            at = pl.multiple_of(which * width + j * TILE, TILE)
            out = jnp.dot(x, w_qkv[layer, :, pl.ds(at, TILE)], preferred_element_type=jnp.float32)
            for part in range(TILE // PAIR):
                cols = out[:, part * PAIR : (part + 1) * PAIR]
                slot = j * (TILE // PAIR) + part
                if which == 1:
                    k_s[slot, pl.ds(row, rows), :] = cols.astype(jnp.bfloat16)
                else:
                    va_s[slot, pl.ds(row, rows), :] = jnp.where(first_half, cols, 1.0).astype(
                        jnp.bfloat16
                    )
                    vb_s[slot, pl.ds(row, rows), :] = jnp.where(first_half, 1.0, cols).astype(
                        jnp.bfloat16
                    )

    def project_q(layer, j):
        at = pl.multiple_of(j * TILE, TILE)
        x = states[layer, pl.ds(AT_OWN, tok_rows), :]
        out = jnp.dot(x, w_qkv[layer, :, pl.ds(at, TILE)], preferred_element_type=jnp.float32)
        out = out * (0.125 * LOG2E)
        for part in range(TILE // PAIR):
            cols = out[:, part * PAIR : (part + 1) * PAIR]
            slot = j * (TILE // PAIR) + part
            qa = jnp.where(first_half, cols, 0.0).astype(jnp.bfloat16)
            qb = jnp.where(first_half, 0.0, cols).astype(jnp.bfloat16)
            for block in range(tok_rows // BLOCK):
                rows = slice(block * BLOCK, (block + 1) * BLOCK)
                q_s[slot, block, pl.ds(0, BLOCK), :] = qa[rows]
                q_s[slot, block, pl.ds(BLOCK, BLOCK), :] = qb[rows]

    def score(block, pair, parts):
        band = AT_BEFORE + block * BLOCK
        scores = []
        for which in parts:
            start = AT_PROMPT if which == 0 else band + (which - 1) * BLOCK
            s = lax.dot_general(
                q_s[pair, block],
                k_s[pair, pl.ds(start, BLOCK), :],
                (((1,), (1,)), ((), ())),
                preferred_element_type=jnp.float32,
            )
            if which != 2:
                bias = bias_s[block, min(which, 2)]
                s = jnp.concatenate([s[:BLOCK] + bias, s[BLOCK:] + bias], axis=0)
            scores.append(s)
        return scores

    def weigh(block, pair, parts, scores, top, out_a, out_b):
        band = AT_BEFORE + block * BLOCK
        for which, s in zip(parts, scores):
            start = AT_PROMPT if which == 0 else band + (which - 1) * BLOCK
            p = jnp.exp2((s - top).astype(jnp.bfloat16))
            more_a = jnp.dot(
                p[:BLOCK], va_s[pair, pl.ds(start, BLOCK), :], preferred_element_type=jnp.float32
            )
            more_b = jnp.dot(
                p[BLOCK:], vb_s[pair, pl.ds(start, BLOCK), :], preferred_element_type=jnp.float32
            )
            out_a = more_a if out_a is None else out_a + more_a
            out_b = more_b if out_b is None else out_b + more_b
        return out_a, out_b

    def row_top(scores):
        return jnp.max(functools.reduce(jnp.maximum, scores), axis=-1, keepdims=True)

    def finish(pair, out_a, out_b):
        total = pltpu.roll(jnp.where(first_half, out_b, out_a), HEAD, 1)
        att = jnp.where(first_half, out_a, out_b) / total
        att_s[:, pl.ds(pl.multiple_of(pair * PAIR, PAIR), PAIR)] = att.astype(jnp.bfloat16)

    def in_groups(block, parts, use, size=GROUP):
        def step(group):
            members = [group * size + i for i in range(size)]
            scores = score(block, members[0], parts)
            for i, pair in enumerate(members):
                ahead = score(block, members[i + 1], parts) if i + 1 < size else None
                use(pair, scores)
                scores = ahead

        return step

    def attend(block):
        parts = (0, 1, 2, 3)

        def use(pair, scores):
            finish(pair, *weigh(block, pair, parts, scores, row_top(scores), None, None))

        return in_groups(block, parts, use)

    def attend_band(block):
        parts = (1, 2, 3)

        def use(pair, scores):
            top = row_top(scores)
            out_a, out_b = weigh(block, pair, parts, scores, top, None, None)
            part_s[pair, 0] = out_a
            part_s[pair, 1] = out_b
            top_s[pair] = jnp.broadcast_to(top, (2 * BLOCK, PAIR))

        return in_groups(block, parts, use, BAND_GROUP)

    def attend_prompt(block):
        parts = (0,)

        def use(pair, scores):
            before = top_s[pair][:, :1]
            top = jnp.maximum(before, row_top(scores))
            scale = jnp.exp2(before - top)
            out_a = part_s[pair, 0] * scale[:BLOCK]
            out_b = part_s[pair, 1] * scale[BLOCK:]
            finish(pair, *weigh(block, pair, parts, scores, top, out_a, out_b))

        return in_groups(block, parts, use)

    def add_out(layer, block):
        rows = pl.ds(block * BLOCK, BLOCK)
        source = hidden_ref if layer == 0 else h_s
        old = source[rows, :].astype(jnp.float32)
        new = old + jnp.dot(att_s[...], w_out[layer], preferred_element_type=jnp.float32)
        return new.astype(jnp.bfloat16)

    def head(block, h):
        rows = pl.ds(block * BLOCK, BLOCK)
        final = norm_rows(h.astype(jnp.float32), final_gain_ref[...].reshape(1, width))
        out = jnp.dot(final, w_heads[...], preferred_element_type=jnp.float32)
        logits, table = out[:, :ACTIONS], out[:, ACTIONS:]
        exps = jnp.exp(logits - jnp.max(logits, axis=-1, keepdims=True))
        norm = jnp.sum(exps, axis=-1, keepdims=True)
        action = jnp.broadcast_to(actions_ref[:, rows].astype(jnp.float32), (128, BLOCK))
        action = jnp.transpose(action)[:, :1].astype(jnp.int32)
        chosen = action == lax.broadcasted_iota(jnp.int32, (1, ACTIONS), 1)
        reward = jnp.sum(jnp.where(chosen, table, 0.0), axis=-1, keepdims=True)
        prob = jnp.sum(jnp.where(chosen, exps, 0.0), axis=-1, keepdims=True) / norm
        direct = jnp.sum(exps * table, axis=-1, keepdims=True) / norm
        place = lax.broadcasted_iota(jnp.int32, (1, 128), 1)
        packed = jnp.where(place == 0, reward, jnp.where(place == 1, prob, direct))
        packed = jnp.transpose(packed)
        reward, prob, direct = packed[0:1], packed[1:2], packed[2:3]
        logged_prob = propensity_ref[:, rows].astype(jnp.float32) / 65536.0
        cutoff = 0.5 * switch_ref[0].astype(jnp.float32)
        weight = jnp.minimum(prob / logged_prob, cutoff)
        out_ref[0:1, rows] = reward
        out_ref[1:2, rows] = direct + weight * (logged_ref[:, rows] - reward)

    def own_block(block):
        return pl.ds(AT_OWN + block * BLOCK, BLOCK)

    for block in range(2):
        rows = hidden_ref[pl.ds(block * BLOCK, BLOCK), :].astype(jnp.float32)
        states[0, own_block(block), :] = norm_rows(rows, gain_ref[0:1, :])

    count = jnp.int32(0)
    for _, there in partners:
        count = count + jnp.where(there, 1, 0)
    pl.semaphore_wait(barrier, count)

    start_prompt(0)
    send_halo(0, 0)
    send_halo(0, 1)

    @pl.when(jnp.logical_not(has_left))
    def _():
        for layer in range(LAYERS):
            states[layer, pl.ds(AT_BEFORE, HALF), :] = jnp.zeros((HALF, width), jnp.bfloat16)

    @pl.when(jnp.logical_not(has_right))
    def _():
        for layer in range(LAYERS):
            states[layer, pl.ds(at_after, HALF), :] = jnp.zeros((HALF, width), jnp.bfloat16)

    row = lax.broadcasted_iota(jnp.int32, (BLOCK, BLOCK), 0)
    col = lax.broadcasted_iota(jnp.int32, (BLOCK, BLOCK), 1)
    for block in range(2):
        place = me * 2 + block
        off = row - col
        seen = (
            off + place * BLOCK > HALF,
            (off <= 0) & (place > 0),
            (off >= 0) & (place < 2 * n - 1),
        )
        for which, ok in enumerate(seen):
            bias_s[block, which] = jnp.where(ok, 0.0, -1e30)

    loads[0].wait()

    @pl.loop(0, tiles)
    def _(j):
        pass_on(0, j - (tiles - 2))
        project_kv(0, AT_OWN, tok_rows, j)
        project_q(0, j)

    wait_halo(0, 0)

    @pl.loop(0, tiles)
    def _(j):
        project_kv(0, at_after, HALF, j)

    wait_halo(0, 1)

    @pl.loop(0, tiles)
    def _(j):
        project_kv(0, AT_BEFORE, HALF, j)

    groups, band_groups = pairs // GROUP, pairs // BAND_GROUP
    band_step, prompt_step, second_step = attend_band(0), attend_prompt(0), attend(1)

    @pl.loop(0, band_groups)
    def _(group):
        pass_on(0, group + 2)
        band_step(group)

    finish_passing(0, 2 + band_groups)

    @pl.loop(0, tiles)
    def _(j):
        project_kv(0, AT_PROMPT, PROMPT, j)

    @pl.loop(0, groups)
    def _(group):
        prompt_step(group)

    loads[1].wait()
    h = add_out(0, 0)
    h_s[pl.ds(0, BLOCK), :] = h
    states[1, own_block(0), :] = norm_rows(h.astype(jnp.float32), gain_ref[1:2, :])
    send_halo(1, 0)
    start_prompt(1)

    @pl.loop(0, groups)
    def _(group):
        pass_on(1, group)
        second_step(group)

    h = add_out(0, 1)
    h_s[pl.ds(BLOCK, BLOCK), :] = h
    states[1, own_block(1), :] = norm_rows(h.astype(jnp.float32), gain_ref[1:2, :])
    send_halo(1, 1)

    pass_on(1, groups)
    loads[2].wait()

    @pl.loop(0, tiles)
    def _(j):
        project_kv(1, AT_OWN, tok_rows, j)
        project_q(1, j)

    wait_halo(1, 0)

    @pl.loop(0, tiles)
    def _(j):
        project_kv(1, at_after, HALF, j)

    band_step, prompt_step, first_step = attend_band(1), attend_prompt(1), attend(0)

    @pl.loop(0, band_groups)
    def _(group):
        pass_on(1, group + groups + 1)
        band_step(group)

    finish_passing(1, groups + 1 + band_groups)

    @pl.loop(0, tiles)
    def _(j):
        project_kv(1, AT_PROMPT, PROMPT, j)

    @pl.loop(0, groups)
    def _(group):
        prompt_step(group)

    loads[3].wait()
    loads[4].wait()
    head(1, add_out(1, 1))
    wait_halo(1, 1)

    @pl.loop(0, tiles)
    def _(j):
        project_kv(1, AT_BEFORE, HALF, j)

    @pl.loop(0, groups)
    def _(group):
        first_step(group)

    head(0, add_out(1, 0))

    for layer in range(LAYERS):
        for side, there in ((0, has_left), (1, has_right)):

            @pl.when(there)
            def _(layer=layer, side=side):
                halo(layer, side).wait_send()

        for slot, (child, there) in enumerate(children):

            @pl.when(there)
            def _(layer=layer, slot=slot, child=child):
                for chunk in range(CHUNKS):
                    piece(layer, chunk, slot, child).wait_send()


def per_device(
    hidden_in,
    ln_gain,
    w_qkv,
    w_out,
    final_gain,
    w_heads,
    actions,
    propensity,
    logged_reward,
    switch_index,
):
    n = lax.axis_size("seq")
    tok_rows, width = hidden_in.shape
    gathered = tok_rows + 2 * HALF + PROMPT
    pairs = HEADS // 2
    vmem = pl.BlockSpec(memory_space=pltpu.VMEM)
    smem = pl.BlockSpec(memory_space=pltpu.SMEM)
    hbm = pl.BlockSpec(memory_space=pl.ANY)
    bf16 = jnp.bfloat16
    out = pl.pallas_call(
        functools.partial(kernel, n),
        out_shape=jax.ShapeDtypeStruct((2, tok_rows), jnp.float32),
        in_specs=[vmem] * 6 + [smem] + [hbm] * 3,
        out_specs=vmem,
        scratch_shapes=[
            pltpu.VMEM(w_qkv.shape, bf16),
            pltpu.VMEM(w_out.shape, bf16),
            pltpu.VMEM(w_heads.shape, bf16),
            pltpu.VMEM((LAYERS, gathered, width), bf16),
            pltpu.VMEM((pairs, tok_rows // BLOCK, 2 * BLOCK, PAIR), bf16),
            pltpu.VMEM((pairs, gathered, PAIR), bf16),
            pltpu.VMEM((pairs, gathered, PAIR), bf16),
            pltpu.VMEM((pairs, gathered, PAIR), bf16),
            pltpu.VMEM((BLOCK, width), bf16),
            pltpu.VMEM((tok_rows, width), bf16),
            pltpu.VMEM((tok_rows // BLOCK, 3, BLOCK, BLOCK), jnp.float32),
            pltpu.VMEM((pairs, 2, BLOCK, PAIR), jnp.float32),
            pltpu.VMEM((pairs, 2 * BLOCK, PAIR), jnp.float32),
            pltpu.SemaphoreType.DMA((5,)),
            pltpu.SemaphoreType.DMA((LAYERS, 2)),
            pltpu.SemaphoreType.DMA((LAYERS, 2)),
            pltpu.SemaphoreType.DMA((LAYERS, 3, CHUNKS)),
            pltpu.SemaphoreType.DMA((LAYERS, CHUNKS)),
        ],
        compiler_params=pltpu.CompilerParams(
            collective_id=0, has_side_effects=True, vmem_limit_bytes=56 * 2**20
        ),
    )(
        hidden_in,
        ln_gain,
        final_gain,
        actions.reshape(1, tok_rows),
        propensity.reshape(1, tok_rows),
        logged_reward.reshape(1, tok_rows),
        switch_index,
        w_qkv,
        w_out,
        w_heads,
    )
    return out[0], out[1]


def solution(mesh):
    placed = (
        P(("groups", "seq"), None),
        P(),
        P(),
        P(),
        P(),
        P(),
        P(("groups", "seq")),
        P(("groups", "seq")),
        P(("groups", "seq")),
        P("groups"),
    )
    return jax.shard_map(
        per_device,
        mesh=mesh,
        in_specs=placed,
        out_specs=(P(("groups", "seq")), P(("groups", "seq"))),
        check_vma=False,
    )
```

```python
import functools

import jax
import jax.numpy as jnp
from jax import lax
from jax.experimental import pallas as pl
from jax.experimental.pallas import tpu as pltpu
from jax.sharding import PartitionSpec as P

HEADS = 12
HEAD = 64
HALF = 256
PROMPT = 256
ACTIONS = 256
LAYERS = 2
BLOCK = 256
TILE = 256
PAIR = 2 * HEAD
CHUNKS = 4
GROUP = 3
LOCAL_GROUP = 2
MESH = pl.DeviceIdType.MESH
AT_PROMPT, AT_BEFORE, AT_OWN = 0, PROMPT, PROMPT + HALF
LOG2E = 1.4426950408889634


def norm_rows(rows, gain_row):
    row_mean = jnp.mean(rows, axis=-1, keepdims=True)
    centred = rows - row_mean
    row_var = jnp.mean(centred * centred, axis=-1, keepdims=True)
    return (centred * lax.rsqrt(row_var + 1e-05) * gain_row).astype(jnp.bfloat16)


def kernel(
    n,
    hidden_ref,
    gain_ref,
    final_gain_ref,
    actions_ref,
    propensity_ref,
    logged_ref,
    switch_ref,
    w_qkv_hbm,
    w_out_hbm,
    w_heads_hbm,
    out_ref,
    w_qkv,
    w_out,
    w_heads,
    states,
    q_s,
    k_s,
    va_s,
    vb_s,
    att_s,
    h_s,
    bias_s,
    part_s,
    top_s,
    load_sem,
    halo_send,
    halo_recv,
    tree_send,
    tree_recv,
):
    tok_rows, width = hidden_ref.shape
    at_after = AT_OWN + tok_rows
    tiles = width // TILE
    pairs = HEADS // 2
    me = lax.axis_index("seq")
    chip, core = me // 2, me % 2
    points = 2 * ((n // 2 - 1) // 2) + 2
    turn = jnp.where(core == 1, points - 1, jnp.where(chip % 2 == 1, points - 2, chip - 1))
    parent = jnp.where(core == 1, me - 1, jnp.where(chip % 2 == 1, me - 2, me - 4))
    even = core == 0
    children = (
        (me + 4, even & (chip % 2 == 0) & (me + 4 < n)),
        (me + 2, even & (chip % 2 == 0) & (me + 2 < n)),
        (me + 1, even & (me + 1 < n)),
    )
    has_left, has_right, has_parent = me > 0, me < n - 1, me > 0

    loads = [pltpu.make_async_copy(w_qkv_hbm.at[0], w_qkv.at[0], load_sem.at[0])]
    loads.append(pltpu.make_async_copy(w_out_hbm.at[0], w_out.at[0], load_sem.at[1]))
    loads.append(pltpu.make_async_copy(w_qkv_hbm.at[1], w_qkv.at[1], load_sem.at[2]))
    loads.append(pltpu.make_async_copy(w_out_hbm.at[1], w_out.at[1], load_sem.at[3]))
    loads.append(pltpu.make_async_copy(w_heads_hbm, w_heads, load_sem.at[4]))
    for load in loads:
        load.start()

    barrier = pltpu.get_barrier_semaphore()
    partners = ((me - 1, has_left), (me + 1, has_right), (parent, has_parent)) + children
    for partner, there in partners:

        @pl.when(there)
        def _(partner=partner):
            pl.semaphore_signal(barrier, inc=1, device_id={"seq": partner}, device_id_type=MESH)

    def halo(layer, side):
        src = AT_OWN if side == 0 else at_after - HALF
        dst = at_after if side == 0 else AT_BEFORE
        return pltpu.make_async_remote_copy(
            src_ref=states.at[layer, pl.ds(src, HALF)],
            dst_ref=states.at[layer, pl.ds(dst, HALF)],
            send_sem=halo_send.at[layer, side],
            recv_sem=halo_recv.at[layer, side],
            device_id={"seq": me - 1 if side == 0 else me + 1},
            device_id_type=MESH,
        )

    def piece(layer, chunk, slot, target):
        rows = PROMPT // CHUNKS
        part = states.at[layer, pl.ds(pl.multiple_of(chunk * rows, rows), rows)]
        return pltpu.make_async_remote_copy(
            src_ref=part,
            dst_ref=part,
            send_sem=tree_send.at[layer, slot, chunk],
            recv_sem=tree_recv.at[layer, chunk],
            device_id={"seq": target},
            device_id_type=MESH,
        )

    def send_piece(layer, chunk):
        for slot, (child, there) in enumerate(children):

            @pl.when(there)
            def _(slot=slot, child=child):
                piece(layer, chunk, slot, child).start()

    def pass_on(layer, point):
        @pl.when(has_parent & (turn == point))
        def _():
            @pl.loop(0, CHUNKS)
            def _(chunk):
                piece(layer, chunk, 0, parent).wait_recv()
                send_piece(layer, chunk)

    def finish_passing(layer, done):
        if done < points:

            @pl.loop(done, points)
            def _(point):
                pass_on(layer, point)

    def wait_halo(layer, side):
        @pl.when(has_right if side == 0 else has_left)
        def _():
            halo(layer, side).wait_recv()

    def send_halo(layer, side):
        @pl.when(has_left if side == 0 else has_right)
        def _():
            halo(layer, side).start()

    def start_prompt(layer):
        @pl.when(me == 0)
        def _():
            states[layer, pl.ds(AT_PROMPT, PROMPT), :] = states[layer, pl.ds(AT_OWN, PROMPT), :]

            @pl.loop(0, CHUNKS)
            def _(chunk):
                send_piece(layer, chunk)

    lane = lax.broadcasted_iota(jnp.int32, (1, PAIR), 1)
    first_half = lane < HEAD

    def project_kv(layer, row, rows, j):
        x = states[layer, pl.ds(row, rows), :]
        for which in (1, 2):
            at = pl.multiple_of(which * width + j * TILE, TILE)
            out = jnp.dot(x, w_qkv[layer, :, pl.ds(at, TILE)], preferred_element_type=jnp.float32)
            for part in range(TILE // PAIR):
                cols = out[:, part * PAIR : (part + 1) * PAIR]
                slot = j * (TILE // PAIR) + part
                if which == 1:
                    k_s[slot, pl.ds(row, rows), :] = cols.astype(jnp.bfloat16)
                else:
                    va_s[slot, pl.ds(row, rows), :] = jnp.where(first_half, cols, 1.0).astype(
                        jnp.bfloat16
                    )
                    vb_s[slot, pl.ds(row, rows), :] = jnp.where(first_half, 1.0, cols).astype(
                        jnp.bfloat16
                    )

    def project_q(layer, j):
        at = pl.multiple_of(j * TILE, TILE)
        x = states[layer, pl.ds(AT_OWN, tok_rows), :]
        out = jnp.dot(x, w_qkv[layer, :, pl.ds(at, TILE)], preferred_element_type=jnp.float32)
        out = out * (0.125 * LOG2E)
        for part in range(TILE // PAIR):
            cols = out[:, part * PAIR : (part + 1) * PAIR]
            slot = j * (TILE // PAIR) + part
            qa = jnp.where(first_half, cols, 0.0).astype(jnp.bfloat16)
            qb = jnp.where(first_half, 0.0, cols).astype(jnp.bfloat16)
            for block in range(tok_rows // BLOCK):
                rows = slice(block * BLOCK, (block + 1) * BLOCK)
                q_s[slot, block, pl.ds(0, BLOCK), :] = qa[rows]
                q_s[slot, block, pl.ds(BLOCK, BLOCK), :] = qb[rows]

    def score(block, pair, parts):
        band = AT_BEFORE + block * BLOCK
        scores = []
        for which in parts:
            start = AT_PROMPT if which == 0 else band + (which - 1) * BLOCK
            s = lax.dot_general(
                q_s[pair, block],
                k_s[pair, pl.ds(start, BLOCK), :],
                (((1,), (1,)), ((), ())),
                preferred_element_type=jnp.float32,
            )
            if which != 2:
                bias = bias_s[block, min(which, 2)]
                s = jnp.concatenate([s[:BLOCK] + bias, s[BLOCK:] + bias], axis=0)
            scores.append(s)
        return scores

    def weigh(block, pair, parts, scores, top, out_a, out_b):
        band = AT_BEFORE + block * BLOCK
        for which, s in zip(parts, scores):
            start = AT_PROMPT if which == 0 else band + (which - 1) * BLOCK
            p = jnp.exp2((s - top).astype(jnp.bfloat16))
            more_a = jnp.dot(
                p[:BLOCK], va_s[pair, pl.ds(start, BLOCK), :], preferred_element_type=jnp.float32
            )
            more_b = jnp.dot(
                p[BLOCK:], vb_s[pair, pl.ds(start, BLOCK), :], preferred_element_type=jnp.float32
            )
            out_a = more_a if out_a is None else out_a + more_a
            out_b = more_b if out_b is None else out_b + more_b
        return out_a, out_b

    def row_top(scores):
        return jnp.max(functools.reduce(jnp.maximum, scores), axis=-1, keepdims=True)

    def finish(pair, out_a, out_b):
        total = pltpu.roll(jnp.where(first_half, out_b, out_a), HEAD, 1)
        att = jnp.where(first_half, out_a, out_b) / total
        att_s[:, pl.ds(pl.multiple_of(pair * PAIR, PAIR), PAIR)] = att.astype(jnp.bfloat16)

    def in_groups(block, parts, use, size=GROUP):
        def step(group):
            members = [group * size + i for i in range(size)]
            scores = score(block, members[0], parts)
            for i, pair in enumerate(members):
                ahead = score(block, members[i + 1], parts) if i + 1 < size else None
                use(pair, scores)
                scores = ahead

        return step

    def attend(block):
        parts = (0, 1, 2, 3)

        def use(pair, scores):
            finish(pair, *weigh(block, pair, parts, scores, row_top(scores), None, None))

        return in_groups(block, parts, use)

    def attend_local(block):
        parts = (2, 3) if block == 0 else (1, 2)

        def use(pair, scores):
            top = row_top(scores)
            out_a, out_b = weigh(block, pair, parts, scores, top, None, None)
            part_s[block, pair, 0] = out_a
            part_s[block, pair, 1] = out_b
            top_s[block, pair] = jnp.broadcast_to(top, (2 * BLOCK, PAIR))

        return in_groups(block, parts, use, LOCAL_GROUP)

    def attend_rest(block):
        parts = (0, 1) if block == 0 else (0, 3)

        def use(pair, scores):
            before = top_s[block, pair][:, :1]
            top = jnp.maximum(before, row_top(scores))
            scale = jnp.exp2(before - top)
            out_a = part_s[block, pair, 0] * scale[:BLOCK]
            out_b = part_s[block, pair, 1] * scale[BLOCK:]
            finish(pair, *weigh(block, pair, parts, scores, top, out_a, out_b))

        return in_groups(block, parts, use)

    def add_out(layer, block):
        rows = pl.ds(block * BLOCK, BLOCK)
        source = hidden_ref if layer == 0 else h_s
        old = source[rows, :].astype(jnp.float32)
        new = old + jnp.dot(att_s[...], w_out[layer], preferred_element_type=jnp.float32)
        return new.astype(jnp.bfloat16)

    def head(block, h):
        rows = pl.ds(block * BLOCK, BLOCK)
        final = norm_rows(h.astype(jnp.float32), final_gain_ref[...].reshape(1, width))
        out = jnp.dot(final, w_heads[...], preferred_element_type=jnp.float32)
        logits, table = out[:, :ACTIONS], out[:, ACTIONS:]
        exps = jnp.exp(logits - jnp.max(logits, axis=-1, keepdims=True))
        norm = jnp.sum(exps, axis=-1, keepdims=True)
        action = jnp.broadcast_to(actions_ref[:, rows].astype(jnp.float32), (128, BLOCK))
        action = jnp.transpose(action)[:, :1].astype(jnp.int32)
        chosen = action == lax.broadcasted_iota(jnp.int32, (1, ACTIONS), 1)
        reward = jnp.sum(jnp.where(chosen, table, 0.0), axis=-1, keepdims=True)
        prob = jnp.sum(jnp.where(chosen, exps, 0.0), axis=-1, keepdims=True) / norm
        direct = jnp.sum(exps * table, axis=-1, keepdims=True) / norm
        place = lax.broadcasted_iota(jnp.int32, (1, 128), 1)
        packed = jnp.where(place == 0, reward, jnp.where(place == 1, prob, direct))
        packed = jnp.transpose(packed)
        reward, prob, direct = packed[0:1], packed[1:2], packed[2:3]
        logged_prob = propensity_ref[:, rows].astype(jnp.float32) / 65536.0
        cutoff = 0.5 * switch_ref[0].astype(jnp.float32)
        weight = jnp.minimum(prob / logged_prob, cutoff)
        out_ref[0:1, rows] = reward
        out_ref[1:2, rows] = direct + weight * (logged_ref[:, rows] - reward)

    def own_block(block):
        return pl.ds(AT_OWN + block * BLOCK, BLOCK)

    for block in range(2):
        rows = hidden_ref[pl.ds(block * BLOCK, BLOCK), :].astype(jnp.float32)
        states[0, own_block(block), :] = norm_rows(rows, gain_ref[0:1, :])

    count = jnp.int32(0)
    for _, there in partners:
        count = count + jnp.where(there, 1, 0)
    pl.semaphore_wait(barrier, count)

    start_prompt(0)
    send_halo(0, 0)
    send_halo(0, 1)

    @pl.when(jnp.logical_not(has_left))
    def _():
        for layer in range(LAYERS):
            states[layer, pl.ds(AT_BEFORE, HALF), :] = jnp.zeros((HALF, width), jnp.bfloat16)

    @pl.when(jnp.logical_not(has_right))
    def _():
        for layer in range(LAYERS):
            states[layer, pl.ds(at_after, HALF), :] = jnp.zeros((HALF, width), jnp.bfloat16)

    row = lax.broadcasted_iota(jnp.int32, (BLOCK, BLOCK), 0)
    col = lax.broadcasted_iota(jnp.int32, (BLOCK, BLOCK), 1)
    for block in range(2):
        place = me * 2 + block
        off = row - col
        seen = (
            off + place * BLOCK > HALF,
            (off <= 0) & (place > 0),
            (off >= 0) & (place < 2 * n - 1),
        )
        for which, ok in enumerate(seen):
            bias_s[block, which] = jnp.where(ok, 0.0, -1e30)

    loads[0].wait()

    @pl.loop(0, tiles)
    def _(j):
        project_kv(0, AT_OWN, tok_rows, j)
        project_q(0, j)

    groups, local_groups = pairs // GROUP, pairs // LOCAL_GROUP
    for block in range(2):
        local_step = attend_local(block)

        @pl.loop(0, local_groups)
        def _(group, block=block, local_step=local_step):
            pass_on(0, group + block * local_groups)
            local_step(group)

    wait_halo(0, 1)

    @pl.loop(0, tiles)
    def _(j):
        project_kv(0, AT_BEFORE, HALF, j)

    wait_halo(0, 0)

    @pl.loop(0, tiles)
    def _(j):
        project_kv(0, at_after, HALF, j)

    finish_passing(0, 2 * local_groups)

    @pl.loop(0, tiles)
    def _(j):
        project_kv(0, AT_PROMPT, PROMPT, j)

    rest_first, rest_second = attend_rest(0), attend_rest(1)

    @pl.loop(0, groups)
    def _(group):
        rest_first(group)

    loads[1].wait()
    h = add_out(0, 0)
    h_s[pl.ds(0, BLOCK), :] = h
    states[1, own_block(0), :] = norm_rows(h.astype(jnp.float32), gain_ref[1:2, :])
    send_halo(1, 0)
    start_prompt(1)

    @pl.loop(0, groups)
    def _(group):
        pass_on(1, group)
        rest_second(group)

    h = add_out(0, 1)
    h_s[pl.ds(BLOCK, BLOCK), :] = h
    states[1, own_block(1), :] = norm_rows(h.astype(jnp.float32), gain_ref[1:2, :])
    send_halo(1, 1)

    pass_on(1, groups)
    loads[2].wait()

    @pl.loop(0, tiles)
    def _(j):
        pass_on(1, j + groups + 1)
        project_kv(1, AT_OWN, tok_rows, j)
        project_q(1, j)

    done = groups + 1 + tiles
    local_step, rest_step, first_step = attend_local(1), attend_rest(1), attend(0)

    @pl.loop(0, local_groups)
    def _(group):
        pass_on(1, jnp.where(group == 1, done, 0))
        local_step(group)

    wait_halo(1, 0)

    @pl.loop(0, tiles)
    def _(j):
        project_kv(1, at_after, HALF, j)

    finish_passing(1, done + 1)

    @pl.loop(0, tiles)
    def _(j):
        project_kv(1, AT_PROMPT, PROMPT, j)

    @pl.loop(0, groups)
    def _(group):
        rest_step(group)

    loads[3].wait()
    loads[4].wait()
    head(1, add_out(1, 1))
    wait_halo(1, 1)

    @pl.loop(0, tiles)
    def _(j):
        project_kv(1, AT_BEFORE, HALF, j)

    @pl.loop(0, groups)
    def _(group):
        first_step(group)

    head(0, add_out(1, 0))

    for layer in range(LAYERS):
        for side, there in ((0, has_left), (1, has_right)):

            @pl.when(there)
            def _(layer=layer, side=side):
                halo(layer, side).wait_send()

        for slot, (child, there) in enumerate(children):

            @pl.when(there)
            def _(layer=layer, slot=slot, child=child):
                for chunk in range(CHUNKS):
                    piece(layer, chunk, slot, child).wait_send()


def per_device(
    hidden_in,
    ln_gain,
    w_qkv,
    w_out,
    final_gain,
    w_heads,
    actions,
    propensity,
    logged_reward,
    switch_index,
):
    n = lax.axis_size("seq")
    tok_rows, width = hidden_in.shape
    gathered = tok_rows + 2 * HALF + PROMPT
    pairs = HEADS // 2
    vmem = pl.BlockSpec(memory_space=pltpu.VMEM)
    smem = pl.BlockSpec(memory_space=pltpu.SMEM)
    hbm = pl.BlockSpec(memory_space=pl.ANY)
    bf16 = jnp.bfloat16
    out = pl.pallas_call(
        functools.partial(kernel, n),
        out_shape=jax.ShapeDtypeStruct((2, tok_rows), jnp.float32),
        in_specs=[vmem] * 6 + [smem] + [hbm] * 3,
        out_specs=vmem,
        scratch_shapes=[
            pltpu.VMEM(w_qkv.shape, bf16),
            pltpu.VMEM(w_out.shape, bf16),
            pltpu.VMEM(w_heads.shape, bf16),
            pltpu.VMEM((LAYERS, gathered, width), bf16),
            pltpu.VMEM((pairs, tok_rows // BLOCK, 2 * BLOCK, PAIR), bf16),
            pltpu.VMEM((pairs, gathered, PAIR), bf16),
            pltpu.VMEM((pairs, gathered, PAIR), bf16),
            pltpu.VMEM((pairs, gathered, PAIR), bf16),
            pltpu.VMEM((BLOCK, width), bf16),
            pltpu.VMEM((tok_rows, width), bf16),
            pltpu.VMEM((tok_rows // BLOCK, 3, BLOCK, BLOCK), jnp.float32),
            pltpu.VMEM((tok_rows // BLOCK, pairs, 2, BLOCK, PAIR), jnp.float32),
            pltpu.VMEM((tok_rows // BLOCK, pairs, 2 * BLOCK, PAIR), jnp.float32),
            pltpu.SemaphoreType.DMA((5,)),
            pltpu.SemaphoreType.DMA((LAYERS, 2)),
            pltpu.SemaphoreType.DMA((LAYERS, 2)),
            pltpu.SemaphoreType.DMA((LAYERS, 3, CHUNKS)),
            pltpu.SemaphoreType.DMA((LAYERS, CHUNKS)),
        ],
        compiler_params=pltpu.CompilerParams(
            collective_id=0, has_side_effects=True, vmem_limit_bytes=56 * 2**20
        ),
    )(
        hidden_in,
        ln_gain,
        final_gain,
        actions.reshape(1, tok_rows),
        propensity.reshape(1, tok_rows),
        logged_reward.reshape(1, tok_rows),
        switch_index,
        w_qkv,
        w_out,
        w_heads,
    )
    return out[0], out[1]


def solution(mesh):
    placed = (
        P(("groups", "seq"), None),
        P(),
        P(),
        P(),
        P(),
        P(),
        P(("groups", "seq")),
        P(("groups", "seq")),
        P(("groups", "seq")),
        P("groups"),
    )
    return jax.shard_map(
        per_device,
        mesh=mesh,
        in_specs=placed,
        out_specs=(P(("groups", "seq")), P(("groups", "seq"))),
        check_vma=False,
    )
```
